128 devices in a mesh: rep: 16 (over y, x), tp: 8 (over z, core).
Axes of the slice: x: 4, y: 4, z: 4, core: 2. Of those that a mesh axis runs over, the one named last changes fastest.
Arguments:
- queries: bfloat16 [256, 64, 128], P('rep', 'tp'), may hold values from -8 to 8
- new_kv: bfloat16 [256, 8, 256], P('rep', 'tp'), may hold values from -6 to 6
- parent_cache: bfloat16 [128, 8, 1024, 256], P('rep', 'tp'), may hold values from -8 to 8
- parent_len: int32 [128], replicated, may hold values from 1 to 1023, as said below
- child_parent: int32 [256], replicated, may hold values from 0 to 127, as said below
- out_weight: bfloat16 [8192, 4096], P('tp'), may hold values from -0.0625 to 0.0625
Outputs:
- mixed: bfloat16 [256, 4096], P('rep', 'tp')
The draws below stay inside these ranges and needn't reach their ends.
Inputs may be any that keep to these rules, and one draw needn't show every extreme that they name: `parent_len`: some parent has exactly 1023 positions in use. Among the 16 children of one index of rep (consecutive entries), at most 2 have parents held by any one index of rep (child_parent // 8), and on every index of rep some holder has exactly 2 of them.
All inputs are finite; a program needn't handle non-finite values.
Results may differ from the reference program's by a relative error of at most 0.0055.
Values may be sent and summed in bfloat16 or wider, within the bound.
No kernel may reach another device: no remote copies, remote signals or barrier semaphores. Data moves between devices by JAX's collectives and lax.ppermute only.
A program may use at most 128 MiB of HBM per device.

```python
import jax
import jax.numpy as jnp
from jax import lax

HQ = 64
KVH = 8
HD = 128
DOUT = 4096
L = 1024
P_DEV = 8
C_DEV = 16
MOST = 2
NPAR = 128
CHILDREN = 256


def draw_queries(key, part):
    key = jax.random.fold_in(key, 7)
    values = jnp.clip(jax.random.normal(key, (CHILDREN, HQ, HD), jnp.float32), -6.0, 6.0)
    return values.astype(jnp.bfloat16)


def draw_parent_cache(key, part):
    key = jax.random.fold_in(key, 9)
    block_shape = (NPAR, KVH, L, 2 * HD)
    values = jnp.clip(jax.random.normal(key, block_shape, jnp.float32), -6.0, 6.0)
    return values.astype(jnp.bfloat16)


def draw_parent_len(key, part):
    key = jax.random.fold_in(key, 21)
    lengths = jax.random.randint(key, (NPAR,), 1, L)
    longest = jax.random.randint(jax.random.fold_in(key, 1), (), 0, NPAR)
    return lengths.at[longest].set(L - 1).astype(jnp.int32)


def draw_child_parent(key, part):
    key = jax.random.fold_in(key, 31)
    device_count = NPAR // P_DEV

    def one_device(device_key):
        first_source = jax.random.randint(jax.random.fold_in(device_key, 0), (), 0, device_count)
        source_pool = jnp.arange((device_count - 1) * MOST, dtype=jnp.int32) // MOST
        source_pool = source_pool + (source_pool >= first_source).astype(jnp.int32)
        source_pool = jax.random.permutation(jax.random.fold_in(device_key, 1), source_pool)
        sources = jnp.concatenate([jnp.full((MOST,), first_source, jnp.int32), source_pool[:C_DEV - MOST]])
        sources = jax.random.permutation(jax.random.fold_in(device_key, 2), sources)
        pick_one = jax.random.randint(jax.random.fold_in(device_key, 3), (C_DEV,), 0, P_DEV)
        pick_two = jax.random.randint(jax.random.fold_in(device_key, 4), (C_DEV,), 0, P_DEV)
        return (sources, jnp.minimum(pick_one, pick_two))
    device_keys = jax.random.split(key, device_count)
    sources, slot_pick = jax.vmap(one_device)(device_keys)
    slot_order = jax.random.permutation(jax.random.fold_in(key, 5), P_DEV).astype(jnp.int32)
    slots = slot_order[slot_pick]
    return (sources * P_DEV + slots).reshape(CHILDREN).astype(jnp.int32)


def block_levels(rng, dims, cuts, low, largest):
    def one(axis_at, shards_of):
        draws = jax.random.uniform(jax.random.fold_in(jax.random.fold_in(rng, 6), axis_at), (shards_of,), jnp.float32, low / len(cuts), largest / len(cuts))
        return jnp.repeat(jnp.exp(draws), dims[axis_at] // shards_of).reshape((-1,) + (1,) * (len(dims) - axis_at - 1))

    factor_of = one(*cuts[0])
    for cut in cuts[1:]:
        factor_of = factor_of * one(*cut)
    return factor_of


def bell_draw(own_key, dims, scale, limit, pieces=(), held_as=jnp.bfloat16):
    loudness = block_levels(own_key, dims, pieces, -0.22, 0.18) if pieces else 1.0
    array = jax.random.normal(own_key, dims, jnp.float32) * scale * loudness
    return jnp.minimum(jnp.maximum(array, -limit), limit).astype(held_as)


def setup_inputs(seed: int = 0) -> dict:
    splits = jax.random.split(jax.random.key(seed), 7)
    return {
        "queries": draw_queries(jax.random.fold_in(splits[6], 71), 0),
        "new_kv": bell_draw(splits[1], (CHILDREN, KVH, 2 * HD), 1.0, 6.0, ((0, 16), (1, 8))),
        "parent_cache": draw_parent_cache(jax.random.fold_in(splits[6], 71), 0),
        "parent_len": draw_parent_len(jax.random.fold_in(splits[6], 71), 0),
        "child_parent": draw_child_parent(jax.random.fold_in(splits[6], 71), 0),
        "out_weight": bell_draw(splits[5], (HQ * HD, DOUT), (HQ * HD) ** -0.5, 0.0625, ((0, 8),)),
    }


def fork_caches(new_kv, parent_cache, parent_len, child_parent):
    lengths = parent_len[child_parent]
    row_ids = jnp.arange(L, dtype=jnp.int32)
    inherit_mask = (row_ids[None, :] < lengths[:, None])[:, None, :, None]
    fresh_mask = (row_ids[None, :] == lengths[:, None])[:, None, :, None]
    zero_fill = jnp.zeros((), parent_cache.dtype)
    forked = jnp.where(inherit_mask, parent_cache[child_parent], jnp.where(fresh_mask, new_kv[:, :, None, :], zero_fill))
    return forked, lengths


def attend_child(inputs):
    child_block, query_row, length = inputs
    group_size = HQ // KVH
    key_rows = child_block[:, :, :HD].astype(jnp.float32)
    values = child_block[:, :, HD:].astype(jnp.float32)
    grouped = query_row.astype(jnp.float32).reshape(KVH, group_size, HD)
    scores = jnp.einsum("kgd,ktd->kgt", grouped, key_rows) * (HD ** -0.5)
    visible = jnp.arange(L, dtype=jnp.int32) <= length
    scores = jnp.where(visible[None, None, :], scores, -jnp.inf)
    row_max = jnp.max(scores, axis=-1, keepdims=True)
    weights = jnp.exp(scores - row_max)
    denominator = jnp.sum(weights, axis=-1, keepdims=True)
    rounded = lax.optimization_barrier(weights.astype(jnp.bfloat16)).astype(jnp.float32)
    head_out = jnp.einsum("kgt,ktd->kgd", rounded, values) / denominator
    return head_out.reshape(HQ * HD).astype(jnp.bfloat16)


def reference(queries, new_kv, parent_cache, parent_len, child_parent, out_weight):
    child_cache, lengths = fork_caches(new_kv, parent_cache, parent_len, child_parent)
    head_out = lax.map(attend_child, (child_cache, queries, lengths))
    mixed = jnp.dot(head_out, out_weight, preferred_element_type=jnp.float32).astype(jnp.bfloat16)
    return mixed
```

```python
import functools

import jax
import jax.numpy as jnp
from jax import lax
from jax.experimental import pallas as pl
from jax.experimental.pallas import tpu as pltpu
from jax.sharding import PartitionSpec as P

MOST = 2
ROWS = 16
LANES = 4


def pack_kernel(parents, child_count, place, child_parent, queries, new_kv, packets, pick, seen):
    packets[...] = jnp.zeros_like(packets)
    holders = packets.shape[0] // MOST
    for h in range(holders):
        seen[h] = 0
    head_size = queries.shape[-1]
    base = place[0] * child_count
    row = lax.broadcasted_iota(jnp.int32, (8, head_size), 0)
    pick_row = lax.broadcasted_iota(jnp.int32, pick.shape, 0)
    pick_col = lax.broadcasted_iota(jnp.int32, pick.shape, 1) % (holders * MOST)
    chosen = jnp.zeros(pick.shape, jnp.bool_)
    for c in range(child_count):
        holder = lax.div(child_parent[base + c], parents)
        rank = seen[holder]
        seen[holder] = rank + 1
        slot = holder * MOST + rank
        fresh = new_kv[c].astype(jnp.float32)
        tail = jnp.where(row == 0, fresh[:, :head_size], fresh[:, head_size:])
        packet = jnp.concatenate([queries[c].astype(jnp.float32), tail], axis=0)
        packets[slot] = packet.astype(packets.dtype)
        chosen = chosen | ((pick_row == c) & (pick_col == slot))
    pick[...] = jnp.where(chosen, 1.0, 0.0).astype(pick.dtype)


def attend_kernel(
    parents, child_count, place, child_parent, parent_len, packets, cache_hbm, weight_hbm, out,
    cache, weight, heads, found, cache_sem, weight_sem,
):
    get_cache = pltpu.make_async_copy(cache_hbm, cache, cache_sem)
    get_weight = pltpu.make_async_copy(weight_hbm, weight, weight_sem)
    get_cache.start()
    get_weight.start()
    slots = packets.shape[0]
    reps = slots // MOST
    group, head_size = 8, packets.shape[-1]
    cache_len = cache.shape[1]
    me = place[0]
    heads[...] = jnp.zeros_like(heads)

    for i in range(slots + LANES):
        found[i] = slots * parents
    count = jnp.int32(0)
    for r in range(reps):
        rank = jnp.int32(0)
        for c in range(child_count):
            local = child_parent[r * child_count + c] - me * parents
            found[count] = (r * MOST + rank) * parents + local
            hit = ((local >= 0) & (local < parents)).astype(jnp.int32)
            count = count + hit
            rank = rank + hit
    for i in range(LANES):
        found[count + i] = slots * parents
    get_cache.wait()
    column = lax.broadcasted_iota(jnp.int32, (group, cache_len), 1)

    def some(step, carry):
        for lane in range(LANES):
            entry = found[step * LANES + lane]
            slot, local = lax.div(entry, parents), lax.rem(entry, parents)
            length = parent_len[me * parents + local]
            packet = packets[jnp.minimum(slot, slots - 1)]
            keys = cache[local, :, :head_size]
            values = cache[local, :, head_size:]
            scores = lax.dot_general(
                packet, keys, (((1,), (1,)), ((), ())), preferred_element_type=jnp.float32
            )[:group] * head_size ** (-0.5)
            wide = packet.astype(jnp.float32)
            query, new_key, new_value = wide[:group], wide[group : group + 1], wide[group + 1 : group + 2]
            new_score = jnp.sum(query * new_key, axis=1, keepdims=True) * head_size ** (-0.5)
            scores = jnp.where(column < length, scores, -jnp.inf)
            top = jnp.maximum(jnp.max(scores, axis=1, keepdims=True), new_score)
            weights = jnp.exp(scores - top)
            new_weight = jnp.exp(new_score - top)
            total = jnp.sum(weights, axis=1, keepdims=True) + new_weight
            summed = jnp.dot(
                weights.astype(jnp.bfloat16), values, preferred_element_type=jnp.float32
            )
            summed = summed + new_weight.astype(jnp.bfloat16).astype(jnp.float32) * new_value
            heads[pl.ds(pl.multiple_of(slot * group, group), group), :] = summed / total
        return carry

    lax.fori_loop(0, lax.div(count + LANES - 1, LANES), some, 0)
    left = jnp.concatenate(
        [heads[pl.ds(i, slots, stride=group), :].astype(jnp.bfloat16) for i in range(group)], axis=1
    )
    get_weight.wait()
    part = out.shape[1]
    for i in range(out.shape[0] // slots):
        out[i * slots : (i + 1) * slots, :] = jnp.dot(
            left, weight[:, i * part : (i + 1) * part], preferred_element_type=jnp.float32
        ).astype(out.dtype)


def shards(queries, new_kv, parent_cache, parent_len, child_parent, out_weight):
    reps = lax.axis_size("rep")
    tps = lax.axis_size("tp")
    parents, _, cache_len, width = parent_cache.shape
    child_count, group, head_size = queries.shape
    features = out_weight.shape[1]
    slots = reps * MOST
    place = lax.axis_index("rep").astype(jnp.int32).reshape(1)
    smem = pl.BlockSpec(memory_space=pltpu.SMEM)
    vmem = pl.BlockSpec(memory_space=pltpu.VMEM)
    anywhere = pl.BlockSpec(memory_space=pl.ANY)

    packets, pick = pl.pallas_call(
        functools.partial(pack_kernel, parents, child_count),
        out_shape=(
            jax.ShapeDtypeStruct((slots, ROWS, head_size), jnp.bfloat16),
            jax.ShapeDtypeStruct((child_count, tps * slots), jnp.bfloat16),
        ),
        in_specs=[smem, smem, vmem, vmem],
        out_specs=(vmem, vmem),
        scratch_shapes=[pltpu.SMEM((reps,), jnp.int32)],
    )(place, child_parent, queries, new_kv)
    packets = lax.all_to_all(packets, "rep", split_axis=0, concat_axis=0, tiled=True)

    partial = pl.pallas_call(
        functools.partial(attend_kernel, parents, child_count),
        out_shape=jax.ShapeDtypeStruct((tps * slots, features // tps), jnp.bfloat16),
        in_specs=[smem, smem, smem, vmem, anywhere, anywhere],
        out_specs=vmem,
        scratch_shapes=[
            pltpu.VMEM((parents, cache_len, width), jnp.bfloat16),
            pltpu.VMEM(out_weight.shape, jnp.bfloat16),
            pltpu.VMEM(((slots + 1) * group, head_size), jnp.float32),
            pltpu.SMEM((slots + 2 * LANES,), jnp.int32),
            pltpu.SemaphoreType.DMA,
            pltpu.SemaphoreType.DMA,
        ],
        compiler_params=pltpu.CompilerParams(vmem_limit_bytes=24 * 1024 * 1024),
    )(place, child_parent, parent_len, packets, parent_cache.reshape(parents, cache_len, width), out_weight)

    arrived = lax.all_to_all(partial, ("tp", "rep"), split_axis=0, concat_axis=0, tiled=True)
    return jnp.dot(pick, arrived, preferred_element_type=jnp.float32).astype(jnp.bfloat16)


def solution(mesh):
    placed = (
        P("rep", "tp", None),
        P("rep", "tp", None),
        P("rep", "tp", None, None),
        P(),
        P(),
        P("tp", None),
    )
    return jax.shard_map(
        shards, mesh=mesh, in_specs=placed, out_specs=P("rep", "tp"), check_vma=False
    )
```

```python
import functools

import jax
import jax.numpy as jnp
from jax import lax
from jax.experimental import pallas as pl
from jax.experimental.pallas import tpu as pltpu
from jax.sharding import PartitionSpec as P

MOST = 2
ROWS = 16
GROUP = 8
LENGTHS, COUNTS, EXTRAS, EXTRA_COUNT, PLAN = 64, 72, 80, 127, 128
MIB = 1024 * 1024
NEAR = 6
TOGETHER = 4
WAVES = (0, 2), (2, 5), (5, 8)


def pack_kernel(parents, child_count, place, child_parent, queries, new_kv, packets, pick, seen):
    packets[...] = jnp.zeros_like(packets)
    holders = packets.shape[0] // MOST
    for h in range(holders):
        seen[h] = 0
    head_size = queries.shape[-1]
    base = place[0] * child_count
    row = lax.broadcasted_iota(jnp.int32, (8, head_size), 0)
    pick_row = lax.broadcasted_iota(jnp.int32, pick.shape, 0)
    pick_col = lax.broadcasted_iota(jnp.int32, pick.shape, 1) % (holders * MOST)
    chosen = jnp.zeros(pick.shape, jnp.bool_)
    for c in range(child_count):
        holder = lax.div(child_parent[base + c], parents)
        rank = seen[holder]
        seen[holder] = rank + 1
        slot = holder * MOST + rank
        fresh = new_kv[c : c + 1, :].astype(jnp.float32)
        tail = jnp.where(row == 0, fresh[:, :head_size], fresh[:, head_size:])
        packet = jnp.concatenate([queries[c].astype(jnp.float32), tail], axis=0)
        packets[slot] = packet.astype(packets.dtype)
        chosen = chosen | ((pick_row == c) & (pick_col == slot))
    pick[...] = jnp.where(chosen, 1.0, 0.0).astype(pick.dtype)


def ahead_kernel(
    parents, child_count, slots, place, child_parent, parent_len, cache_hbm, near, plan, hits, near_sem
):
    get_near = pltpu.make_async_copy(cache_hbm.at[pl.ds(0, near.shape[0])], near, near_sem)
    get_near.start()
    base = place[0] * parents
    for i in range(parents * GROUP):
        plan[i] = slots
    for p in range(parents):
        plan[LENGTHS + p] = parent_len[base + p]
        plan[COUNTS + p] = 0
    count = jnp.int32(0)
    for r in range(slots // MOST):
        rank = jnp.int32(0)
        for c in range(child_count):
            local = child_parent[r * child_count + c] - base
            hits[count] = (r * MOST + rank) * parents + local
            hit = ((local >= 0) & (local < parents)).astype(jnp.int32)
            count = count + hit
            rank = rank + hit

    def sort(i, extra):
        slot, local = lax.div(hits[i], parents), lax.rem(hits[i], parents)
        before = plan[COUNTS + local]
        plan[COUNTS + local] = before + 1
        fits = before < GROUP

        @pl.when(fits)
        def _():
            plan[local * GROUP + before] = slot

        @pl.when(jnp.logical_not(fits))
        def _():
            plan[EXTRAS + extra] = hits[i]

        return extra + jnp.where(fits, 0, 1)

    plan[EXTRA_COUNT] = lax.fori_loop(0, count, sort, jnp.int32(0))
    get_near.wait()


def attend(packet_lists, keys, values, lengths, group):
    head_size = keys[0].shape[1]
    scale = head_size ** (-0.5)
    wide = [[x.astype(jnp.float32) for x in packets] for packets in packet_lists]
    query = [jnp.concatenate([w[:group] for w in ws], axis=0) for ws in wide]
    scores = [
        lax.dot_general(q.astype(jnp.bfloat16), k, (((1,), (1,)), ((), ())), preferred_element_type=jnp.float32)
        for q, k in zip(query, keys)
    ]
    new_key = [jnp.concatenate([jnp.broadcast_to(w[group : group + 1], (group, head_size)) for w in ws], axis=0) for ws in wide]
    new_score = [jnp.sum(q * k, axis=1, keepdims=True) for q, k in zip(query, new_key)]
    column = lax.broadcasted_iota(jnp.int32, scores[0].shape, 1)
    scores = [jnp.where(column < n, s, -jnp.inf) for s, n in zip(scores, lengths)]
    top = [jnp.maximum(jnp.max(s, axis=1, keepdims=True), x) for s, x in zip(scores, new_score)]
    weights = [jnp.exp((s - t) * scale) for s, t in zip(scores, top)]
    summed = [
        jnp.dot(w.astype(jnp.bfloat16), v, preferred_element_type=jnp.float32) for w, v in zip(weights, values)
    ]
    new_weight = [jnp.exp((x - t) * scale) for x, t in zip(new_score, top)]
    total = [jnp.sum(w, axis=1, keepdims=True) + x for w, x in zip(weights, new_weight)]
    new_value = [jnp.concatenate([jnp.broadcast_to(w[group + 1 : group + 2], (group, head_size)) for w in ws], axis=0) for ws in wide]
    return [
        (s + x.astype(jnp.bfloat16).astype(jnp.float32) * v) / t
        for s, x, v, t in zip(summed, new_weight, new_value, total)
    ]


def attend_kernel(
    parents, plan_in, packets, near, cache_hbm, weight_hbm, out,
    plan, far, weight, heads, plan_sem, far_sem, weight_sems,
):
    slots = packets.shape[0]
    group, head_size = 8, packets.shape[-1]
    part = out.shape[1]
    parts = out.shape[0] // slots
    near_count = near.shape[0]
    get_far = pltpu.make_async_copy(cache_hbm.at[pl.ds(near_count, parents - near_count)], far, far_sem)
    get_weight = [
        pltpu.make_async_copy(
            weight_hbm.at[:, pl.ds(i * part, part)], weight.at[:, pl.ds(i * part, part)], weight_sems.at[i]
        )
        for i in range(parts)
    ]
    get_plan = pltpu.make_async_copy(plan_in, plan, plan_sem)
    get_plan.start()
    get_far.start()
    for i in range(*WAVES[0]):
        get_weight[i].start()
    get_plan.wait()
    heads[...] = jnp.zeros_like(heads)

    def block(p):
        return (near, p) if p < near_count else (far, p - near_count)

    for first in range(0, parents, TOGETHER):
        if first + TOGETHER > near_count:
            get_far.wait()
        some = range(first, first + TOGETHER)
        places = [[plan[p * GROUP + k] for k in range(GROUP)] for p in some]
        results = attend(
            [[packets[jnp.minimum(at, slots - 1)] for at in spots] for spots in places],
            [block(p)[0][block(p)[1], :, :head_size] for p in some],
            [block(p)[0][block(p)[1], :, head_size:] for p in some],
            [plan[LENGTHS + p] for p in some],
            group,
        )
        for spots, result in zip(places, results):
            for k, at in enumerate(spots):
                heads[pl.ds(pl.multiple_of(at * group, group), group), :] = result[k * group : (k + 1) * group]
        if first == 0:
            for i in range(*WAVES[1]):
                get_weight[i].start()

    for i in range(*WAVES[2]):
        get_weight[i].start()

    def one(keys, at, local):
        return attend([[packets[at]]], [keys[:, :head_size]], [keys[:, head_size:]], [plan[LENGTHS + local]], group)[0]

    def extra(i, carry):
        at, local = lax.div(plan[EXTRAS + i], parents), lax.rem(plan[EXTRAS + i], parents)
        rows = pl.ds(pl.multiple_of(at * group, group), group)

        @pl.when(local < near_count)
        def _():
            heads[rows, :] = one(near[jnp.minimum(local, near_count - 1)], at, local)

        @pl.when(local >= near_count)
        def _():
            heads[rows, :] = one(far[jnp.maximum(local - near_count, 0)], at, local)

        return carry

    lax.fori_loop(0, plan[EXTRA_COUNT], extra, 0)
    left = jnp.concatenate(
        [heads[pl.ds(i, slots, stride=group), :].astype(jnp.bfloat16) for i in range(group)], axis=1
    )
    for i in range(parts):
        get_weight[i].wait()
        out[i * slots : (i + 1) * slots, :] = jnp.dot(
            left, weight[:, i * part : (i + 1) * part], preferred_element_type=jnp.float32
        ).astype(out.dtype)


def shards(queries, new_kv, parent_cache, parent_len, child_parent, out_weight):
    reps = lax.axis_size("rep")
    tps = lax.axis_size("tp")
    parents, _, cache_len, width = parent_cache.shape
    child_count, group, head_size = queries.shape
    features = out_weight.shape[1]
    slots = reps * MOST
    place = lax.axis_index("rep").astype(jnp.int32).reshape(1)
    smem = pl.BlockSpec(memory_space=pltpu.SMEM)
    vmem = pl.BlockSpec(memory_space=pltpu.VMEM)
    anywhere = pl.BlockSpec(memory_space=pl.ANY)

    packets, pick = pl.pallas_call(
        functools.partial(pack_kernel, parents, child_count),
        out_shape=(
            jax.ShapeDtypeStruct((slots, ROWS, head_size), jnp.bfloat16),
            jax.ShapeDtypeStruct((child_count, tps * slots), jnp.bfloat16),
        ),
        in_specs=[smem, smem, vmem, vmem],
        out_specs=(vmem, vmem),
        scratch_shapes=[pltpu.SMEM((reps,), jnp.int32)],
    )(place, child_parent, queries, new_kv.reshape(child_count, width))
    packets = lax.all_to_all(packets, "rep", split_axis=0, concat_axis=0, tiled=True)

    caches = parent_cache.reshape(parents, cache_len, width)
    near, plan = pl.pallas_call(
        functools.partial(ahead_kernel, parents, child_count, slots),
        out_shape=(
            jax.ShapeDtypeStruct((NEAR, cache_len, width), caches.dtype),
            jax.ShapeDtypeStruct((PLAN,), jnp.int32),
        ),
        in_specs=[smem, smem, smem, anywhere],
        out_specs=(vmem, smem),
        scratch_shapes=[pltpu.SMEM((slots + 1,), jnp.int32), pltpu.SemaphoreType.DMA],
        compiler_params=pltpu.CompilerParams(vmem_limit_bytes=50 * MIB),
        cost_estimate=pl.CostEstimate(flops=0, bytes_accessed=8 * MIB, transcendentals=0),
    )(place, child_parent, parent_len, caches)

    partial = pl.pallas_call(
        functools.partial(attend_kernel, parents),
        out_shape=jax.ShapeDtypeStruct((tps * slots, features // tps), jnp.bfloat16),
        in_specs=[anywhere, vmem, vmem, anywhere, anywhere],
        out_specs=vmem,
        scratch_shapes=[
            pltpu.SMEM((PLAN,), jnp.int32),
            pltpu.VMEM((parents - NEAR, cache_len, width), jnp.bfloat16),
            pltpu.VMEM(out_weight.shape, jnp.bfloat16),
            pltpu.VMEM(((slots + 1) * group, head_size), jnp.float32),
            pltpu.SemaphoreType.DMA,
            pltpu.SemaphoreType.DMA,
            pltpu.SemaphoreType.DMA((tps,)),
        ],
        compiler_params=pltpu.CompilerParams(vmem_limit_bytes=50 * MIB),
    )(plan, packets, near, caches, out_weight)

    arrived = lax.all_to_all(partial, ("tp", "rep"), split_axis=0, concat_axis=0, tiled=True)
    return jnp.dot(pick, arrived, preferred_element_type=jnp.float32).astype(jnp.bfloat16)


def solution(mesh):
    placed = (
        P("rep", "tp", None),
        P("rep", "tp", None),
        P("rep", "tp", None, None),
        P(),
        P(),
        P("tp", None),
    )
    return jax.shard_map(
        shards, mesh=mesh, in_specs=placed, out_specs=P("rep", "tp"), check_vma=False
    )
```

```python
import functools

import jax
import jax.numpy as jnp
from jax import lax
from jax.experimental import pallas as pl
from jax.experimental.pallas import tpu as pltpu
from jax.sharding import PartitionSpec as P

MOST = 2
ROWS = 16
GROUP = 8
COUNTS, EXTRAS, EXTRA_COUNT, PLAN = 64, 80, 127, 128
MIB = 1024 * 1024
LOG2_E = 1.4426950408889634
NEAR = 6
STAGES = (0, 1, 2, 3), (4, 5, 6, 7)
WAVES = (0, 2), (2, 5), (5, 8)
LATE = {}


def pack_kernel(parents, child_count, place, child_parent, parent_len, queries, new_kv, packets, pick, seen):
    packets[...] = jnp.zeros_like(packets)
    holders = packets.shape[0] // MOST
    for h in range(holders):
        seen[h] = 0
    head_size = queries.shape[-1]
    base = place[0] * child_count
    row = lax.broadcasted_iota(jnp.int32, (8, head_size), 0)
    pick_row = lax.broadcasted_iota(jnp.int32, pick.shape, 0)
    pick_col = lax.broadcasted_iota(jnp.int32, pick.shape, 1) % (holders * MOST)
    chosen = jnp.zeros(pick.shape, jnp.bool_)
    for c in range(child_count):
        parent = child_parent[base + c]
        holder = lax.div(parent, parents)
        rank = seen[holder]
        seen[holder] = rank + 1
        slot = holder * MOST + rank
        fresh = new_kv[c : c + 1, :].astype(jnp.float32)
        length = parent_len[parent]
        high, low = lax.div(length, 32).astype(jnp.float32), lax.rem(length, 32).astype(jnp.float32)
        tail = jnp.where(row == 0, fresh[:, :head_size], fresh[:, head_size:])
        tail = jnp.where(row < 2, tail, jnp.where(row == 2, high, low))
        packet = jnp.concatenate([queries[c].astype(jnp.float32), tail], axis=0)
        packets[slot] = packet.astype(packets.dtype)
        chosen = chosen | ((pick_row == c) & (pick_col == slot))
    pick[...] = jnp.where(chosen, 1.0, 0.0).astype(pick.dtype)


def ahead_kernel(
    parents, child_count, slots, place, child_parent_in, cache_hbm, near, plan,
    child_parent, hits, near_sem, parent_sem,
):
    get_near = pltpu.make_async_copy(cache_hbm.at[pl.ds(0, near.shape[0])], near, near_sem)
    get_parent = pltpu.make_async_copy(child_parent_in, child_parent, parent_sem)
    get_parent.start()
    get_near.start()
    base = place[0] * parents
    for i in range(parents * GROUP):
        plan[i] = slots
    for p in range(parents):
        plan[COUNTS + p] = 0
    get_parent.wait()
    count = jnp.int32(0)
    for r in range(slots // MOST):
        rank = jnp.int32(0)
        for c in range(child_count):
            local = child_parent[r * child_count + c] - base
            hits[count] = (r * MOST + rank) * parents + local
            hit = ((local >= 0) & (local < parents)).astype(jnp.int32)
            count = count + hit
            rank = rank + hit

    def sort(i, extra):
        slot, local = lax.div(hits[i], parents), lax.rem(hits[i], parents)
        before = plan[COUNTS + local]
        plan[COUNTS + local] = before + 1
        fits = before < GROUP

        @pl.when(fits)
        def _():
            plan[local * GROUP + before] = slot

        @pl.when(jnp.logical_not(fits))
        def _():
            plan[EXTRAS + extra] = hits[i]

        return extra + jnp.where(fits, 0, 1)

    plan[EXTRA_COUNT] = lax.fori_loop(0, count, sort, jnp.int32(0))
    get_near.wait()


def attend(packet_lists, keys, values, group):
    head_size = keys[0].shape[1]
    scale = head_size ** (-0.5) * LOG2_E

    def row_of(packet, i):
        return jnp.broadcast_to(packet[group + i : group + i + 1], (group, head_size))

    wide = [[x.astype(jnp.float32) for x in packets] for packets in packet_lists]
    query = [jnp.concatenate([w[:group] for w in ws], axis=0) for ws in wide]
    scores = [
        lax.dot_general(q.astype(jnp.bfloat16), k, (((1,), (1,)), ((), ())), preferred_element_type=jnp.float32)
        for q, k in zip(query, keys)
    ]
    new_key = [jnp.concatenate([row_of(w, 0) for w in ws], axis=0) for ws in wide]
    new_score = [jnp.sum(q * k, axis=1, keepdims=True) for q, k in zip(query, new_key)]
    column = lax.broadcasted_iota(jnp.int32, (group, scores[0].shape[1]), 1).astype(jnp.float32)
    bias = [jnp.where(column < row_of(ws[0], 2)[:, :1] * 32.0 + row_of(ws[0], 3)[:, :1], 0.0, -jnp.inf) for ws in wide]
    scores = [s + jnp.concatenate([b] * len(ws), axis=0) for s, b, ws in zip(scores, bias, wide)]
    top = [jnp.maximum(jnp.max(s, axis=1, keepdims=True), x) for s, x in zip(scores, new_score)]
    weights = [jnp.exp2((s - t) * scale) for s, t in zip(scores, top)]
    summed = [
        jnp.dot(w.astype(jnp.bfloat16), v, preferred_element_type=jnp.float32) for w, v in zip(weights, values)
    ]
    new_weight = [jnp.exp2((x - t) * scale) for x, t in zip(new_score, top)]
    total = [jnp.sum(w, axis=1, keepdims=True) + x for w, x in zip(weights, new_weight)]
    new_value = [jnp.concatenate([row_of(w, 1) for w in ws], axis=0) for ws in wide]
    return [
        (s + x.astype(jnp.bfloat16).astype(jnp.float32) * v) / t
        for s, x, v, t in zip(summed, new_weight, new_value, total)
    ]


def attend_kernel(
    parents, plan_in, packets, near, cache_hbm, weight_hbm, out,
    plan, far, weight, heads, plan_sem, far_sem, weight_sems,
):
    slots = packets.shape[0]
    group, head_size = 8, packets.shape[-1]
    part = out.shape[1]
    parts = out.shape[0] // slots
    near_count = near.shape[0]
    get_far = pltpu.make_async_copy(cache_hbm.at[pl.ds(near_count, parents - near_count)], far, far_sem)
    get_weight = [
        pltpu.make_async_copy(
            weight_hbm.at[:, pl.ds(i * part, part)], weight.at[:, pl.ds(i * part, part)], weight_sems.at[i]
        )
        for i in range(parts)
    ]
    get_plan = pltpu.make_async_copy(plan_in, plan, plan_sem)
    get_plan.start()
    get_far.start()
    for i in range(*WAVES[0]):
        get_weight[i].start()
    get_plan.wait()
    heads[...] = jnp.zeros_like(heads)

    def block(p):
        return (near, p) if p < near_count else (far, p - near_count)

    for stage, some in enumerate(STAGES):
        if some[-1] == parents - 1:
            get_far.wait()
        places = [[plan[p * GROUP + k] for k in range(GROUP)] for p in some]
        results = attend(
            [[packets[jnp.minimum(at, slots - 1)] for at in spots] for spots in places],
            [block(p)[0][block(p)[1], :, :head_size] for p in some],
            [block(p)[0][block(p)[1], :, head_size:] for p in some],
            group,
        )
        for spots, result in zip(places, results):
            for k, at in enumerate(spots):
                heads[pl.ds(pl.multiple_of(at * group, group), group), :] = result[k * group : (k + 1) * group]
        for i in range(*WAVES[stage + 1]):
            get_weight[i].start()

    def one(keys, at):
        return attend([[packets[at]]], [keys[:, :head_size]], [keys[:, head_size:]], group)[0]

    def extra(i, carry):
        at, local = lax.div(plan[EXTRAS + i], parents), lax.rem(plan[EXTRAS + i], parents)
        rows = pl.ds(pl.multiple_of(at * group, group), group)

        @pl.when(local < near_count)
        def _():
            heads[rows, :] = one(near[jnp.minimum(local, near_count - 1)], at)

        @pl.when(local >= near_count)
        def _():
            heads[rows, :] = one(far[jnp.maximum(local - near_count, 0)], at)

        return carry

    lax.fori_loop(0, plan[EXTRA_COUNT], extra, 0)
    left = jnp.concatenate(
        [heads[pl.ds(i, slots, stride=group), :].astype(jnp.bfloat16) for i in range(group)], axis=1
    )
    for i in range(parts):
        get_weight[i].wait()
        for j in range(*LATE.get(i, (0, 0))):
            get_weight[j].start()
        out[i * slots : (i + 1) * slots, :] = jnp.dot(
            left, weight[:, i * part : (i + 1) * part], preferred_element_type=jnp.float32
        ).astype(out.dtype)


def shards(queries, new_kv, parent_cache, parent_len, child_parent, out_weight):
    reps = lax.axis_size("rep")
    tps = lax.axis_size("tp")
    parents, _, cache_len, width = parent_cache.shape
    child_count, group, head_size = queries.shape
    features = out_weight.shape[1]
    slots = reps * MOST
    place = lax.axis_index("rep").astype(jnp.int32).reshape(1)
    smem = pl.BlockSpec(memory_space=pltpu.SMEM)
    vmem = pl.BlockSpec(memory_space=pltpu.VMEM)
    anywhere = pl.BlockSpec(memory_space=pl.ANY)

    packets, pick = pl.pallas_call(
        functools.partial(pack_kernel, parents, child_count),
        out_shape=(
            jax.ShapeDtypeStruct((slots, ROWS, head_size), jnp.bfloat16),
            jax.ShapeDtypeStruct((child_count, tps * slots), jnp.bfloat16),
        ),
        in_specs=[smem, smem, smem, vmem, vmem],
        out_specs=(vmem, vmem),
        scratch_shapes=[pltpu.SMEM((reps,), jnp.int32)],
    )(place, child_parent, parent_len, queries, new_kv.reshape(child_count, width))
    packets = lax.all_to_all(packets, "rep", split_axis=0, concat_axis=0, tiled=True)

    caches = parent_cache.reshape(parents, cache_len, width)
    near, plan = pl.pallas_call(
        functools.partial(ahead_kernel, parents, child_count, slots),
        out_shape=(
            jax.ShapeDtypeStruct((NEAR, cache_len, width), caches.dtype),
            jax.ShapeDtypeStruct((PLAN,), jnp.int32),
        ),
        in_specs=[smem, anywhere, anywhere],
        out_specs=(vmem, smem),
        scratch_shapes=[
            pltpu.SMEM(child_parent.shape, jnp.int32),
            pltpu.SMEM((slots + 1,), jnp.int32),
            pltpu.SemaphoreType.DMA,
            pltpu.SemaphoreType.DMA,
        ],
        compiler_params=pltpu.CompilerParams(vmem_limit_bytes=50 * MIB),
        cost_estimate=pl.CostEstimate(flops=0, bytes_accessed=8 * MIB, transcendentals=0),
    )(place, child_parent, caches)

    partial = pl.pallas_call(
        functools.partial(attend_kernel, parents),
        out_shape=jax.ShapeDtypeStruct((tps * slots, features // tps), jnp.bfloat16),
        in_specs=[anywhere, vmem, vmem, anywhere, anywhere],
        out_specs=vmem,
        scratch_shapes=[
            pltpu.SMEM((PLAN,), jnp.int32),
            pltpu.VMEM((parents - NEAR, cache_len, width), jnp.bfloat16),
            pltpu.VMEM(out_weight.shape, jnp.bfloat16),
            pltpu.VMEM(((slots + 1) * group, head_size), jnp.float32),
            pltpu.SemaphoreType.DMA,
            pltpu.SemaphoreType.DMA,
            pltpu.SemaphoreType.DMA((tps,)),
        ],
        compiler_params=pltpu.CompilerParams(vmem_limit_bytes=50 * MIB),
    )(plan, packets, near, caches, out_weight)

    arrived = lax.all_to_all(partial, ("tp", "rep"), split_axis=0, concat_axis=0, tiled=True)
    return jnp.dot(pick, arrived, preferred_element_type=jnp.float32).astype(jnp.bfloat16)


def solution(mesh):
    placed = (
        P("rep", "tp", None),
        P("rep", "tp", None),
        P("rep", "tp", None, None),
        P(),
        P(),
        P("tp", None),
    )
    return jax.shard_map(
        shards, mesh=mesh, in_specs=placed, out_specs=P("rep", "tp"), check_vma=False
    )
```

```python
import functools

import jax
import jax.numpy as jnp
from jax import lax
from jax.experimental import pallas as pl
from jax.experimental.pallas import tpu as pltpu
from jax.sharding import PartitionSpec as P

MOST = 2
ROWS = 16
GROUP = 8
COUNTS, EXTRAS, EXTRA_COUNT, PLAN = 64, 80, 127, 128
MIB = 1024 * 1024
LOG2_E = 1.4426950408889634
NEAR = 6
STAGES = (0, 1, 2, 3), (4, 5, 6, 7)
CUTS = (0, 3, 6, 8)


def pack_kernel(parents, child_count, place, child_parent, parent_len, queries, new_kv, packets, pick, seen):
    packets[...] = jnp.zeros_like(packets)
    holders = packets.shape[0] // MOST
    for h in range(holders):
        seen[h] = 0
    head_size = queries.shape[-1]
    base = place[0] * child_count
    row = lax.broadcasted_iota(jnp.int32, (8, head_size), 0)
    pick_row = lax.broadcasted_iota(jnp.int32, pick.shape, 0)
    pick_col = lax.broadcasted_iota(jnp.int32, pick.shape, 1) % (holders * MOST)
    chosen = jnp.zeros(pick.shape, jnp.bool_)
    for c in range(child_count):
        parent = child_parent[base + c]
        holder = lax.div(parent, parents)
        rank = seen[holder]
        seen[holder] = rank + 1
        slot = holder * MOST + rank
        fresh = new_kv[c : c + 1, :].astype(jnp.float32)
        length = parent_len[parent]
        high, low = lax.div(length, 32).astype(jnp.float32), lax.rem(length, 32).astype(jnp.float32)
        tail = jnp.where(row == 0, fresh[:, :head_size], fresh[:, head_size:])
        tail = jnp.where(row < 2, tail, jnp.where(row == 2, high, low))
        packet = jnp.concatenate([queries[c].astype(jnp.float32), tail], axis=0)
        packets[slot] = packet.astype(packets.dtype)
        chosen = chosen | ((pick_row == c) & (pick_col == slot))
    pick[...] = jnp.where(chosen, 1.0, 0.0).astype(pick.dtype)


def ahead_kernel(
    parents, child_count, slots, place, child_parent_in, cache_hbm, near, plan,
    child_parent, hits, near_sem, parent_sem,
):
    get_near = pltpu.make_async_copy(cache_hbm.at[pl.ds(0, near.shape[0])], near, near_sem)
    get_parent = pltpu.make_async_copy(child_parent_in, child_parent, parent_sem)
    get_parent.start()
    get_near.start()
    base = place[0] * parents
    for i in range(parents * GROUP):
        plan[i] = slots
    for p in range(parents):
        plan[COUNTS + p] = 0
    get_parent.wait()
    count = jnp.int32(0)
    for r in range(slots // MOST):
        rank = jnp.int32(0)
        for c in range(child_count):
            local = child_parent[r * child_count + c] - base
            hits[count] = (r * MOST + rank) * parents + local
            hit = ((local >= 0) & (local < parents)).astype(jnp.int32)
            count = count + hit
            rank = rank + hit

    def sort(i, extra):
        slot, local = lax.div(hits[i], parents), lax.rem(hits[i], parents)
        before = plan[COUNTS + local]
        plan[COUNTS + local] = before + 1
        fits = before < GROUP

        @pl.when(fits)
        def _():
            plan[local * GROUP + before] = slot

        @pl.when(jnp.logical_not(fits))
        def _():
            plan[EXTRAS + extra] = hits[i]

        return extra + jnp.where(fits, 0, 1)

    plan[EXTRA_COUNT] = lax.fori_loop(0, count, sort, jnp.int32(0))
    get_near.wait()


def attend(packet_lists, keys, values, group):
    head_size = keys[0].shape[1]
    scale = head_size ** (-0.5) * LOG2_E

    def row_of(packet, i):
        return jnp.broadcast_to(packet[group + i : group + i + 1], (group, head_size))

    wide = [[x.astype(jnp.float32) for x in packets] for packets in packet_lists]
    query = [jnp.concatenate([w[:group] for w in ws], axis=0) for ws in wide]
    scores = [
        lax.dot_general(q.astype(jnp.bfloat16), k, (((1,), (1,)), ((), ())), preferred_element_type=jnp.float32)
        for q, k in zip(query, keys)
    ]
    new_key = [jnp.concatenate([row_of(w, 0) for w in ws], axis=0) for ws in wide]
    new_score = [jnp.sum(q * k, axis=1, keepdims=True) for q, k in zip(query, new_key)]
    column = lax.broadcasted_iota(jnp.int32, (group, scores[0].shape[1]), 1).astype(jnp.float32)
    bias = [jnp.where(column < row_of(ws[0], 2)[:, :1] * 32.0 + row_of(ws[0], 3)[:, :1], 0.0, -jnp.inf) for ws in wide]
    scores = [s + jnp.concatenate([b] * len(ws), axis=0) for s, b, ws in zip(scores, bias, wide)]
    top = [jnp.maximum(jnp.max(s, axis=1, keepdims=True), x) for s, x in zip(scores, new_score)]
    weights = [jnp.exp2((s - t) * scale) for s, t in zip(scores, top)]
    summed = [
        jnp.dot(w.astype(jnp.bfloat16), v, preferred_element_type=jnp.float32) for w, v in zip(weights, values)
    ]
    new_weight = [jnp.exp2((x - t) * scale) for x, t in zip(new_score, top)]
    total = [jnp.sum(w, axis=1, keepdims=True) + x for w, x in zip(weights, new_weight)]
    new_value = [jnp.concatenate([row_of(w, 1) for w in ws], axis=0) for ws in wide]
    return [
        (s + x.astype(jnp.bfloat16).astype(jnp.float32) * v) / t
        for s, x, v, t in zip(summed, new_weight, new_value, total)
    ]


def attend_kernel(
    parents, plan_in, packets, near, cache_hbm, weight_hbm, out,
    plan, far, weight, heads, plan_sem, far_sem, weight_sems,
):
    slots = packets.shape[0]
    group, head_size = 8, packets.shape[-1]
    part = out.shape[1]
    parts = out.shape[0] // slots
    near_count = near.shape[0]
    get_far = pltpu.make_async_copy(cache_hbm.at[pl.ds(near_count, parents - near_count)], far, far_sem)
    bounds = [(cut * part, after * part) for cut, after in zip(CUTS, CUTS[1:])]
    get_weight = [
        pltpu.make_async_copy(
            weight_hbm.at[:, pl.ds(cut, after - cut)], weight.at[:, pl.ds(cut, after - cut)], weight_sems.at[i]
        )
        for i, (cut, after) in enumerate(bounds)
    ]
    get_plan = pltpu.make_async_copy(plan_in, plan, plan_sem)
    get_plan.start()
    get_far.start()
    for copy in get_weight:
        copy.start(priority=1)
    get_plan.wait()
    heads[...] = jnp.zeros_like(heads)

    def block(p):
        return (near, p) if p < near_count else (far, p - near_count)

    for some in STAGES:
        if some[-1] == parents - 1:
            get_far.wait()
        places = [[plan[p * GROUP + k] for k in range(GROUP)] for p in some]
        results = attend(
            [[packets[jnp.minimum(at, slots - 1)] for at in spots] for spots in places],
            [block(p)[0][block(p)[1], :, :head_size] for p in some],
            [block(p)[0][block(p)[1], :, head_size:] for p in some],
            group,
        )
        for spots, result in zip(places, results):
            for k, at in enumerate(spots):
                heads[pl.ds(pl.multiple_of(at * group, group), group), :] = result[k * group : (k + 1) * group]
    def one(keys, at):
        return attend([[packets[at]]], [keys[:, :head_size]], [keys[:, head_size:]], group)[0]

    def extra(i, carry):
        at, local = lax.div(plan[EXTRAS + i], parents), lax.rem(plan[EXTRAS + i], parents)
        rows = pl.ds(pl.multiple_of(at * group, group), group)

        @pl.when(local < near_count)
        def _():
            heads[rows, :] = one(near[jnp.minimum(local, near_count - 1)], at)

        @pl.when(local >= near_count)
        def _():
            heads[rows, :] = one(far[jnp.maximum(local - near_count, 0)], at)

        return carry

    lax.fori_loop(0, plan[EXTRA_COUNT], extra, 0)
    left = jnp.concatenate(
        [heads[pl.ds(i, slots, stride=group), :].astype(jnp.bfloat16) for i in range(group)], axis=1
    )
    for i in range(parts):
        if i in CUTS:
            get_weight[CUTS.index(i)].wait()
        out[i * slots : (i + 1) * slots, :] = jnp.dot(
            left, weight[:, i * part : (i + 1) * part], preferred_element_type=jnp.float32
        ).astype(out.dtype)


def shards(queries, new_kv, parent_cache, parent_len, child_parent, out_weight):
    reps = lax.axis_size("rep")
    tps = lax.axis_size("tp")
    parents, _, cache_len, width = parent_cache.shape
    child_count, group, head_size = queries.shape
    features = out_weight.shape[1]
    slots = reps * MOST
    place = lax.axis_index("rep").astype(jnp.int32).reshape(1)
    smem = pl.BlockSpec(memory_space=pltpu.SMEM)
    vmem = pl.BlockSpec(memory_space=pltpu.VMEM)
    anywhere = pl.BlockSpec(memory_space=pl.ANY)

    packets, pick = pl.pallas_call(
        functools.partial(pack_kernel, parents, child_count),
        out_shape=(
            jax.ShapeDtypeStruct((slots, ROWS, head_size), jnp.bfloat16),
            jax.ShapeDtypeStruct((child_count, tps * slots), jnp.bfloat16),
        ),
        in_specs=[smem, smem, smem, vmem, vmem],
        out_specs=(vmem, vmem),
        scratch_shapes=[pltpu.SMEM((reps,), jnp.int32)],
    )(place, child_parent, parent_len, queries, new_kv.reshape(child_count, width))
    packets = lax.all_to_all(packets, "rep", split_axis=0, concat_axis=0, tiled=True)

    caches = parent_cache.reshape(parents, cache_len, width)
    near, plan = pl.pallas_call(
        functools.partial(ahead_kernel, parents, child_count, slots),
        out_shape=(
            jax.ShapeDtypeStruct((NEAR, cache_len, width), caches.dtype),
            jax.ShapeDtypeStruct((PLAN,), jnp.int32),
        ),
        in_specs=[smem, anywhere, anywhere],
        out_specs=(vmem, smem),
        scratch_shapes=[
            pltpu.SMEM(child_parent.shape, jnp.int32),
            pltpu.SMEM((slots + 1,), jnp.int32),
            pltpu.SemaphoreType.DMA,
            pltpu.SemaphoreType.DMA,
        ],
        compiler_params=pltpu.CompilerParams(vmem_limit_bytes=50 * MIB),
        cost_estimate=pl.CostEstimate(flops=0, bytes_accessed=8 * MIB, transcendentals=0),
    )(place, child_parent, caches)

    partial = pl.pallas_call(
        functools.partial(attend_kernel, parents),
        out_shape=jax.ShapeDtypeStruct((tps * slots, features // tps), jnp.bfloat16),
        in_specs=[anywhere, vmem, vmem, anywhere, anywhere],
        out_specs=vmem,
        scratch_shapes=[
            pltpu.SMEM((PLAN,), jnp.int32),
            pltpu.VMEM((parents - NEAR, cache_len, width), jnp.bfloat16),
            pltpu.VMEM(out_weight.shape, jnp.bfloat16),
            pltpu.VMEM(((slots + 1) * group, head_size), jnp.float32),
            pltpu.SemaphoreType.DMA,
            pltpu.SemaphoreType.DMA,
            pltpu.SemaphoreType.DMA((len(CUTS) - 1,)),
        ],
        compiler_params=pltpu.CompilerParams(vmem_limit_bytes=50 * MIB),
    )(plan, packets, near, caches, out_weight)

    arrived = lax.all_to_all(partial, ("tp", "rep"), split_axis=0, concat_axis=0, tiled=True)
    return jnp.dot(pick, arrived, preferred_element_type=jnp.float32).astype(jnp.bfloat16)


def solution(mesh):
    placed = (
        P("rep", "tp", None),
        P("rep", "tp", None),
        P("rep", "tp", None, None),
        P(),
        P(),
        P("tp", None),
    )
    return jax.shard_map(
        shards, mesh=mesh, in_specs=placed, out_specs=P("rep", "tp"), check_vma=False
    )
```

```python
import functools

import jax
import jax.numpy as jnp
from jax import lax
from jax.experimental import pallas as pl
from jax.experimental.pallas import tpu as pltpu
from jax.sharding import PartitionSpec as P

MOST = 2
ROWS = 8
BLOCKS = MOST + 1
EXTRA_ROWS = 4
GROUP = 8
COUNTS, EXTRAS, EXTRA_COUNT, PLAN = 64, 80, 127, 128
MIB = 1024 * 1024
LOG2_E = 1.4426950408889634
NEAR = 6
STAGES = (0, 1, 2, 3), (4, 5, 6, 7)
CUTS = (0, 3, 6, 8)


def pack_kernel(parents, child_count, place, child_parent, parent_len, queries, new_kv, packets, pick, seen, tails):
    packets[...] = jnp.zeros_like(packets)
    tails[...] = jnp.zeros_like(tails)
    holders = packets.shape[0] // BLOCKS
    for h in range(holders):
        seen[h] = 0
    head_size = queries.shape[-1]
    base = place[0] * child_count
    row = lax.broadcasted_iota(jnp.int32, (ROWS, head_size), 0)
    pick_row = lax.broadcasted_iota(jnp.int32, pick.shape, 0)
    pick_col = lax.broadcasted_iota(jnp.int32, pick.shape, 1) % (holders * MOST)
    chosen = jnp.zeros(pick.shape, jnp.bool_)
    for c in range(child_count):
        parent = child_parent[base + c]
        holder = lax.div(parent, parents)
        rank = seen[holder]
        seen[holder] = rank + 1
        slot = holder * MOST + rank
        fresh = new_kv[c : c + 1, :].astype(jnp.float32)
        length = parent_len[parent]
        high, low = lax.div(length, 32).astype(jnp.float32), lax.rem(length, 32).astype(jnp.float32)
        at = row - rank * EXTRA_ROWS
        tail = jnp.where(at == 0, fresh[:, :head_size], fresh[:, head_size:])
        tail = jnp.where(at < 2, tail, jnp.where(at == 2, high, low))
        tails[holder] = jnp.where((at >= 0) & (at < EXTRA_ROWS), tail, tails[holder])
        packets[holder * BLOCKS + rank] = queries[c]
        chosen = chosen | ((pick_row == c) & (pick_col == slot))
    pick[...] = jnp.where(chosen, 1.0, 0.0).astype(pick.dtype)
    for h in range(holders):
        packets[h * BLOCKS + MOST] = tails[h].astype(packets.dtype)


def ahead_kernel(
    parents, child_count, slots, place, child_parent_in, cache_hbm, near, plan,
    child_parent, hits, near_sem, parent_sem,
):
    get_near = pltpu.make_async_copy(cache_hbm.at[pl.ds(0, near.shape[0])], near, near_sem)
    get_parent = pltpu.make_async_copy(child_parent_in, child_parent, parent_sem)
    get_parent.start()
    get_near.start()
    for i in range(parents * GROUP):
        plan[i] = slots
    for p in range(parents):
        plan[COUNTS + p] = 0
    get_parent.wait()
    held = slots // MOST * parents
    count = jnp.int32(0)
    for r in range(slots // MOST):
        for c in range(child_count):
            parent = child_parent[r * child_count + c]
            hits[count] = parent + r * held
            count = count + (lax.div(parent, parents) == place[0]).astype(jnp.int32)

    def sort(i, carry):
        extra, last, rank = carry
        rep, local = lax.div(hits[i], held), lax.rem(hits[i], parents)
        rank = jnp.where(rep == last, rank + 1, 0)
        slot = rep * MOST + rank
        before = plan[COUNTS + local]
        plan[COUNTS + local] = before + 1
        fits = before < GROUP
        plan[jnp.where(fits, local * GROUP + before, EXTRAS + extra)] = jnp.where(fits, slot, slot * parents + local)
        return extra + jnp.where(fits, 0, 1), rep, rank

    start = (jnp.int32(0), jnp.int32(-1), jnp.int32(0))
    plan[EXTRA_COUNT] = lax.fori_loop(0, count, sort, start)[0]
    get_near.wait()


def unpack(packets, slot):
    holder, rank = lax.div(slot, MOST), lax.rem(slot, MOST)
    query = packets[holder * BLOCKS + rank].astype(jnp.float32)
    tail = packets[holder * BLOCKS + MOST].astype(jnp.float32)
    rows = [
        jnp.where(rank == 0, tail[i : i + 1], tail[i + EXTRA_ROWS : i + EXTRA_ROWS + 1]) for i in range(EXTRA_ROWS)
    ]
    return query, rows


def attend(packet_lists, keys, values, group):
    head_size = keys[0].shape[1]
    scale = head_size ** (-0.5) * LOG2_E

    def row_of(child, i):
        return jnp.broadcast_to(child[1][i], (group, head_size))

    wide = packet_lists
    query = [jnp.concatenate([w[0] for w in ws], axis=0) for ws in wide]
    scores = [
        lax.dot_general(q.astype(jnp.bfloat16), k, (((1,), (1,)), ((), ())), preferred_element_type=jnp.float32)
        for q, k in zip(query, keys)
    ]
    new_key = [jnp.concatenate([row_of(w, 0) for w in ws], axis=0) for ws in wide]
    new_score = [jnp.sum(q * k, axis=1, keepdims=True) for q, k in zip(query, new_key)]
    column = lax.broadcasted_iota(jnp.int32, (group, scores[0].shape[1]), 1).astype(jnp.float32)
    bias = [jnp.where(column < row_of(ws[0], 2)[:, :1] * 32.0 + row_of(ws[0], 3)[:, :1], 0.0, -jnp.inf) for ws in wide]
    scores = [s + jnp.concatenate([b] * len(ws), axis=0) for s, b, ws in zip(scores, bias, wide)]
    top = [jnp.maximum(jnp.max(s, axis=1, keepdims=True), x) for s, x in zip(scores, new_score)]
    weights = [jnp.exp2((s - t) * scale) for s, t in zip(scores, top)]
    summed = [
        jnp.dot(w.astype(jnp.bfloat16), v, preferred_element_type=jnp.float32) for w, v in zip(weights, values)
    ]
    new_weight = [jnp.exp2((x - t) * scale) for x, t in zip(new_score, top)]
    total = [jnp.sum(w, axis=1, keepdims=True) + x for w, x in zip(weights, new_weight)]
    new_value = [jnp.concatenate([row_of(w, 1) for w in ws], axis=0) for ws in wide]
    return [
        (s + x.astype(jnp.bfloat16).astype(jnp.float32) * v) / t
        for s, x, v, t in zip(summed, new_weight, new_value, total)
    ]


def attend_kernel(
    parents, plan_in, packets, near, cache_hbm, weight_hbm, out,
    plan, far, weight, heads, plan_sem, far_sem, weight_sems,
):
    slots = packets.shape[0] // BLOCKS * MOST
    group, head_size = packets.shape[1:]
    part = out.shape[1]
    parts = out.shape[0] // slots
    near_count = near.shape[0]
    get_far = pltpu.make_async_copy(cache_hbm.at[pl.ds(near_count, parents - near_count)], far, far_sem)
    bounds = [(cut * part, after * part) for cut, after in zip(CUTS, CUTS[1:])]
    get_weight = [
        pltpu.make_async_copy(
            weight_hbm.at[:, pl.ds(cut, after - cut)], weight.at[:, pl.ds(cut, after - cut)], weight_sems.at[i]
        )
        for i, (cut, after) in enumerate(bounds)
    ]
    get_plan = pltpu.make_async_copy(plan_in, plan, plan_sem)
    get_plan.start()
    get_far.start()
    for copy in get_weight:
        copy.start(priority=1)
    get_plan.wait()
    heads[...] = jnp.zeros_like(heads)

    def block(p):
        return (near, p) if p < near_count else (far, p - near_count)

    for some in STAGES:
        if some[-1] == parents - 1:
            get_far.wait()
        places = [[plan[p * GROUP + k] for k in range(GROUP)] for p in some]
        results = attend(
            [[unpack(packets, jnp.minimum(at, slots - 1)) for at in spots] for spots in places],
            [block(p)[0][block(p)[1], :, :head_size] for p in some],
            [block(p)[0][block(p)[1], :, head_size:] for p in some],
            group,
        )
        for spots, result in zip(places, results):
            for k, at in enumerate(spots):
                heads[pl.ds(pl.multiple_of(at * group, group), group), :] = result[k * group : (k + 1) * group]
    def one(keys, at):
        return attend([[unpack(packets, at)]], [keys[:, :head_size]], [keys[:, head_size:]], group)[0]

    def extra(i, carry):
        at, local = lax.div(plan[EXTRAS + i], parents), lax.rem(plan[EXTRAS + i], parents)
        rows = pl.ds(pl.multiple_of(at * group, group), group)

        @pl.when(local < near_count)
        def _():
            heads[rows, :] = one(near[jnp.minimum(local, near_count - 1)], at)

        @pl.when(local >= near_count)
        def _():
            heads[rows, :] = one(far[jnp.maximum(local - near_count, 0)], at)

        return carry

    lax.fori_loop(0, plan[EXTRA_COUNT], extra, 0)
    left = jnp.concatenate(
        [heads[pl.ds(i, slots, stride=group), :].astype(jnp.bfloat16) for i in range(group)], axis=1
    )
    for i in range(parts):
        if i in CUTS:
            get_weight[CUTS.index(i)].wait()
        out[i * slots : (i + 1) * slots, :] = jnp.dot(
            left, weight[:, i * part : (i + 1) * part], preferred_element_type=jnp.float32
        ).astype(out.dtype)


def shards(queries, new_kv, parent_cache, parent_len, child_parent, out_weight):
    reps = lax.axis_size("rep")
    tps = lax.axis_size("tp")
    parents, _, cache_len, width = parent_cache.shape
    child_count, group, head_size = queries.shape
    features = out_weight.shape[1]
    slots = reps * MOST
    place = lax.axis_index("rep").astype(jnp.int32).reshape(1)
    smem = pl.BlockSpec(memory_space=pltpu.SMEM)
    vmem = pl.BlockSpec(memory_space=pltpu.VMEM)
    anywhere = pl.BlockSpec(memory_space=pl.ANY)

    packets, pick = pl.pallas_call(
        functools.partial(pack_kernel, parents, child_count),
        out_shape=(
            jax.ShapeDtypeStruct((reps * BLOCKS, ROWS, head_size), jnp.bfloat16),
            jax.ShapeDtypeStruct((child_count, tps * slots), jnp.bfloat16),
        ),
        in_specs=[smem, smem, smem, vmem, vmem],
        out_specs=(vmem, vmem),
        scratch_shapes=[pltpu.SMEM((reps,), jnp.int32), pltpu.VMEM((reps, ROWS, head_size), jnp.float32)],
    )(place, child_parent, parent_len, queries, new_kv.reshape(child_count, width))
    packets = lax.all_to_all(packets, "rep", split_axis=0, concat_axis=0, tiled=True)

    caches = parent_cache.reshape(parents, cache_len, width)
    near, plan = pl.pallas_call(
        functools.partial(ahead_kernel, parents, child_count, slots),
        out_shape=(
            jax.ShapeDtypeStruct((NEAR, cache_len, width), caches.dtype),
            jax.ShapeDtypeStruct((PLAN,), jnp.int32),
        ),
        in_specs=[smem, anywhere, anywhere],
        out_specs=(vmem, smem),
        scratch_shapes=[
            pltpu.SMEM(child_parent.shape, jnp.int32),
            pltpu.SMEM((slots + 1,), jnp.int32),
            pltpu.SemaphoreType.DMA,
            pltpu.SemaphoreType.DMA,
        ],
        compiler_params=pltpu.CompilerParams(vmem_limit_bytes=50 * MIB),
        cost_estimate=pl.CostEstimate(flops=0, bytes_accessed=8 * MIB, transcendentals=0),
    )(place, child_parent, caches)

    partial = pl.pallas_call(
        functools.partial(attend_kernel, parents),
        out_shape=jax.ShapeDtypeStruct((tps * slots, features // tps), jnp.bfloat16),
        in_specs=[anywhere, vmem, vmem, anywhere, anywhere],
        out_specs=vmem,
        scratch_shapes=[
            pltpu.SMEM((PLAN,), jnp.int32),
            pltpu.VMEM((parents - NEAR, cache_len, width), jnp.bfloat16),
            pltpu.VMEM(out_weight.shape, jnp.bfloat16),
            pltpu.VMEM(((slots + 1) * group, head_size), jnp.float32),
            pltpu.SemaphoreType.DMA,
            pltpu.SemaphoreType.DMA,
            pltpu.SemaphoreType.DMA((len(CUTS) - 1,)),
        ],
        compiler_params=pltpu.CompilerParams(vmem_limit_bytes=50 * MIB),
    )(plan, packets, near, caches, out_weight)

    arrived = lax.all_to_all(partial, ("tp", "rep"), split_axis=0, concat_axis=0, tiled=True)
    return jnp.dot(pick, arrived, preferred_element_type=jnp.float32).astype(jnp.bfloat16)


def solution(mesh):
    placed = (
        P("rep", "tp", None),
        P("rep", "tp", None),
        P("rep", "tp", None, None),
        P(),
        P(),
        P("tp", None),
    )
    return jax.shard_map(
        shards, mesh=mesh, in_specs=placed, out_specs=P("rep", "tp"), check_vma=False
    )
```

```python
import functools

import jax
import jax.numpy as jnp
from jax import lax
from jax.experimental import pallas as pl
from jax.experimental.pallas import tpu as pltpu
from jax.sharding import PartitionSpec as P

MOST = 2
ROWS = 8
BLOCKS = MOST + 1
EXTRA_ROWS = 4
GROUP = 8
COUNTS, EXTRAS, EXTRA_COUNT, PLAN = 64, 80, 127, 128
MIB = 1024 * 1024
LOG2_E = 1.4426950408889634
NEAR = 6
STAGES = (0, 1, 2, 3), (4, 5, 6, 7)
CUTS = (0, 4, 6, 8)
WIDE = 2


def pack_kernel(parents, child_count, place, child_parent, parent_len, queries, new_kv, packets, pick, seen, tails):
    packets[...] = jnp.zeros_like(packets)
    tails[...] = jnp.zeros_like(tails)
    holders = packets.shape[0] // BLOCKS
    for h in range(holders):
        seen[h] = 0
    head_size = queries.shape[-1]
    base = place[0] * child_count
    row = lax.broadcasted_iota(jnp.int32, (ROWS, head_size), 0)
    pick_row = lax.broadcasted_iota(jnp.int32, pick.shape, 0)
    pick_col = lax.broadcasted_iota(jnp.int32, pick.shape, 1) % (holders * MOST)
    chosen = jnp.zeros(pick.shape, jnp.bool_)
    for c in range(child_count):
        parent = child_parent[base + c]
        holder = lax.div(parent, parents)
        rank = seen[holder]
        seen[holder] = rank + 1
        slot = holder * MOST + rank
        fresh = new_kv[c : c + 1, :].astype(jnp.float32)
        length = parent_len[parent]
        high, low = lax.div(length, 32).astype(jnp.float32), lax.rem(length, 32).astype(jnp.float32)
        at = row - rank * EXTRA_ROWS
        tail = jnp.where(at == 0, fresh[:, :head_size], fresh[:, head_size:])
        tail = jnp.where(at < 2, tail, jnp.where(at == 2, high, low))
        tails[holder] = jnp.where((at >= 0) & (at < EXTRA_ROWS), tail, tails[holder])
        packets[holder * BLOCKS + rank] = queries[c]
        chosen = chosen | ((pick_row == c) & (pick_col == slot))
    pick[...] = jnp.where(chosen, 1.0, 0.0).astype(pick.dtype)
    for h in range(holders):
        packets[h * BLOCKS + MOST] = tails[h].astype(packets.dtype)


def ahead_kernel(
    parents, child_count, slots, place, child_parent_in, cache_hbm, near, plan,
    child_parent, hits, near_sem, parent_sem,
):
    get_near = pltpu.make_async_copy(cache_hbm.at[pl.ds(0, near.shape[0])], near, near_sem)
    get_parent = pltpu.make_async_copy(child_parent_in, child_parent, parent_sem)
    get_parent.start()
    get_near.start()
    for i in range(parents * GROUP):
        plan[i] = slots
    for p in range(parents):
        plan[COUNTS + p] = 0
    get_parent.wait()
    held = slots // MOST * parents
    count = jnp.int32(0)
    for r in range(slots // MOST):
        for c in range(child_count):
            parent = child_parent[r * child_count + c]
            hits[count] = parent + r * held
            count = count + (lax.div(parent, parents) == place[0]).astype(jnp.int32)

    def sort(i, carry):
        extra, last, rank = carry
        rep, local = lax.div(hits[i], held), lax.rem(hits[i], parents)
        rank = jnp.where(rep == last, rank + 1, 0)
        slot = rep * MOST + rank
        before = plan[COUNTS + local]
        plan[COUNTS + local] = before + 1
        fits = before < GROUP
        plan[jnp.where(fits, local * GROUP + before, EXTRAS + extra)] = jnp.where(fits, slot, slot * parents + local)
        return extra + jnp.where(fits, 0, 1), rep, rank

    start = (jnp.int32(0), jnp.int32(-1), jnp.int32(0))
    plan[EXTRA_COUNT] = lax.fori_loop(0, count, sort, start)[0]
    get_near.wait()


def unpack(packets, slot):
    holder, rank = lax.div(slot, MOST), lax.rem(slot, MOST)
    query = packets[holder * BLOCKS + rank].astype(jnp.float32)
    tail = packets[holder * BLOCKS + MOST].astype(jnp.float32)
    rows = [
        jnp.where(rank == 0, tail[i : i + 1], tail[i + EXTRA_ROWS : i + EXTRA_ROWS + 1]) for i in range(EXTRA_ROWS)
    ]
    return query, rows


def attend(packet_lists, keys, values, group):
    head_size = keys[0].shape[1]
    scale = head_size ** (-0.5) * LOG2_E

    def row_of(child, i):
        return jnp.broadcast_to(child[1][i], (group, head_size))

    wide = packet_lists
    query = [jnp.concatenate([w[0] for w in ws], axis=0) for ws in wide]
    scores = [
        lax.dot_general(q.astype(jnp.bfloat16), k, (((1,), (1,)), ((), ())), preferred_element_type=jnp.float32)
        for q, k in zip(query, keys)
    ]
    new_key = [jnp.concatenate([row_of(w, 0) for w in ws], axis=0) for ws in wide]
    new_score = [jnp.sum(q * k, axis=1, keepdims=True) for q, k in zip(query, new_key)]
    column = lax.broadcasted_iota(jnp.int32, (group, scores[0].shape[1]), 1).astype(jnp.float32)
    bias = [jnp.where(column < row_of(ws[0], 2)[:, :1] * 32.0 + row_of(ws[0], 3)[:, :1], 0.0, -jnp.inf) for ws in wide]
    scores = [s + jnp.concatenate([b] * len(ws), axis=0) for s, b, ws in zip(scores, bias, wide)]
    top = [jnp.maximum(jnp.max(s, axis=1, keepdims=True), x) for s, x in zip(scores, new_score)]
    weights = [jnp.exp2((s - t) * scale) for s, t in zip(scores, top)]
    summed = [
        jnp.dot(w.astype(jnp.bfloat16), v, preferred_element_type=jnp.float32) for w, v in zip(weights, values)
    ]
    new_weight = [jnp.exp2((x - t) * scale) for x, t in zip(new_score, top)]
    total = [jnp.sum(w, axis=1, keepdims=True) + x for w, x in zip(weights, new_weight)]
    new_value = [jnp.concatenate([row_of(w, 1) for w in ws], axis=0) for ws in wide]
    return [
        (s + x.astype(jnp.bfloat16).astype(jnp.float32) * v) / t
        for s, x, v, t in zip(summed, new_weight, new_value, total)
    ]


def attend_kernel(
    parents, plan_in, packets, near, cache_hbm, weight_hbm, out,
    plan, far, weight, heads, plan_sem, far_sem, weight_sems,
):
    slots = packets.shape[0] // BLOCKS * MOST
    group, head_size = packets.shape[1:]
    part = out.shape[1]
    parts = out.shape[0] // slots
    near_count = near.shape[0]
    get_far = pltpu.make_async_copy(cache_hbm.at[pl.ds(near_count, parents - near_count)], far, far_sem)
    bounds = [(cut * part, after * part) for cut, after in zip(CUTS, CUTS[1:])]
    get_weight = [
        pltpu.make_async_copy(
            weight_hbm.at[:, pl.ds(cut, after - cut)], weight.at[:, pl.ds(cut, after - cut)], weight_sems.at[i]
        )
        for i, (cut, after) in enumerate(bounds)
    ]
    get_plan = pltpu.make_async_copy(plan_in, plan, plan_sem)
    get_plan.start()
    get_far.start()
    for copy in get_weight:
        copy.start(priority=1)
    get_plan.wait()
    heads[...] = jnp.zeros_like(heads)

    def block(p):
        return (near, p) if p < near_count else (far, p - near_count)

    for some in STAGES:
        if some[-1] == parents - 1:
            get_far.wait()
        places = [[plan[p * GROUP + k] for k in range(GROUP)] for p in some]
        results = attend(
            [[unpack(packets, jnp.minimum(at, slots - 1)) for at in spots] for spots in places],
            [block(p)[0][block(p)[1], :, :head_size] for p in some],
            [block(p)[0][block(p)[1], :, head_size:] for p in some],
            group,
        )
        for spots, result in zip(places, results):
            for k, at in enumerate(spots):
                heads[pl.ds(pl.multiple_of(at * group, group), group), :] = result[k * group : (k + 1) * group]
    def one(keys, at):
        return attend([[unpack(packets, at)]], [keys[:, :head_size]], [keys[:, head_size:]], group)[0]

    def extra(i, carry):
        at, local = lax.div(plan[EXTRAS + i], parents), lax.rem(plan[EXTRAS + i], parents)
        rows = pl.ds(pl.multiple_of(at * group, group), group)

        @pl.when(local < near_count)
        def _():
            heads[rows, :] = one(near[jnp.minimum(local, near_count - 1)], at)

        @pl.when(local >= near_count)
        def _():
            heads[rows, :] = one(far[jnp.maximum(local - near_count, 0)], at)

        return carry

    lax.fori_loop(0, plan[EXTRA_COUNT], extra, 0)
    left = jnp.concatenate(
        [heads[pl.ds(i, slots, stride=group), :].astype(jnp.bfloat16) for i in range(group)], axis=1
    )
    for copy, (cut, after) in zip(get_weight, bounds):
        copy.wait()
        for low in range(cut, after, WIDE * part):
            sums = jnp.dot(left, weight[:, low : low + WIDE * part], preferred_element_type=jnp.float32).astype(out.dtype)
            for i in range(WIDE):
                first = (low // part + i) * slots
                out[first : first + slots, :] = sums[:, i * part : (i + 1) * part]


def shards(queries, new_kv, parent_cache, parent_len, child_parent, out_weight):
    reps = lax.axis_size("rep")
    tps = lax.axis_size("tp")
    parents, _, cache_len, width = parent_cache.shape
    child_count, group, head_size = queries.shape
    features = out_weight.shape[1]
    slots = reps * MOST
    place = lax.axis_index("rep").astype(jnp.int32).reshape(1)
    smem = pl.BlockSpec(memory_space=pltpu.SMEM)
    vmem = pl.BlockSpec(memory_space=pltpu.VMEM)
    anywhere = pl.BlockSpec(memory_space=pl.ANY)

    packets, pick = pl.pallas_call(
        functools.partial(pack_kernel, parents, child_count),
        out_shape=(
            jax.ShapeDtypeStruct((reps * BLOCKS, ROWS, head_size), jnp.bfloat16),
            jax.ShapeDtypeStruct((child_count, tps * slots), jnp.bfloat16),
        ),
        in_specs=[smem, smem, smem, vmem, vmem],
        out_specs=(vmem, vmem),
        scratch_shapes=[pltpu.SMEM((reps,), jnp.int32), pltpu.VMEM((reps, ROWS, head_size), jnp.float32)],
    )(place, child_parent, parent_len, queries, new_kv.reshape(child_count, width))
    packets = lax.all_to_all(packets, "rep", split_axis=0, concat_axis=0, tiled=True)

    caches = parent_cache.reshape(parents, cache_len, width)
    near, plan = pl.pallas_call(
        functools.partial(ahead_kernel, parents, child_count, slots),
        out_shape=(
            jax.ShapeDtypeStruct((NEAR, cache_len, width), caches.dtype),
            jax.ShapeDtypeStruct((PLAN,), jnp.int32),
        ),
        in_specs=[smem, anywhere, anywhere],
        out_specs=(vmem, smem),
        scratch_shapes=[
            pltpu.SMEM(child_parent.shape, jnp.int32),
            pltpu.SMEM((slots + 1,), jnp.int32),
            pltpu.SemaphoreType.DMA,
            pltpu.SemaphoreType.DMA,
        ],
        compiler_params=pltpu.CompilerParams(vmem_limit_bytes=50 * MIB),
        cost_estimate=pl.CostEstimate(flops=0, bytes_accessed=8 * MIB, transcendentals=0),
    )(place, child_parent, caches)

    partial = pl.pallas_call(
        functools.partial(attend_kernel, parents),
        out_shape=jax.ShapeDtypeStruct((tps * slots, features // tps), jnp.bfloat16),
        in_specs=[anywhere, vmem, vmem, anywhere, anywhere],
        out_specs=vmem,
        scratch_shapes=[
            pltpu.SMEM((PLAN,), jnp.int32),
            pltpu.VMEM((parents - NEAR, cache_len, width), jnp.bfloat16),
            pltpu.VMEM(out_weight.shape, jnp.bfloat16),
            pltpu.VMEM(((slots + 1) * group, head_size), jnp.float32),
            pltpu.SemaphoreType.DMA,
            pltpu.SemaphoreType.DMA,
            pltpu.SemaphoreType.DMA((len(CUTS) - 1,)),
        ],
        compiler_params=pltpu.CompilerParams(vmem_limit_bytes=50 * MIB),
    )(plan, packets, near, caches, out_weight)

    arrived = lax.all_to_all(partial, ("tp", "rep"), split_axis=0, concat_axis=0, tiled=True)
    return jnp.dot(pick, arrived, preferred_element_type=jnp.float32).astype(jnp.bfloat16)


def solution(mesh):
    placed = (
        P("rep", "tp", None),
        P("rep", "tp", None),
        P("rep", "tp", None, None),
        P(),
        P(),
        P("tp", None),
    )
    return jax.shard_map(
        shards, mesh=mesh, in_specs=placed, out_specs=P("rep", "tp"), check_vma=False
    )
```

```python
import functools

import jax
import jax.numpy as jnp
from jax import lax
from jax.experimental import pallas as pl
from jax.experimental.pallas import tpu as pltpu
from jax.sharding import PartitionSpec as P

MOST = 2
ROWS = 8
BLOCKS = MOST + 1
EXTRA_ROWS = 4
GROUP = 8
COUNTS, EXTRAS, EXTRA_COUNT, PLAN = 64, 80, 127, 128
MIB = 1024 * 1024
LOG2_E = 1.4426950408889634
NEAR = 6
STAGES = (0, 1, 2, 3, 4, 5), (6, 7)
CUTS = (0, 4, 6, 8)
WIDE = 2


def pack_kernel(parents, child_count, place, child_parent, parent_len, queries, new_kv, packets, pick, seen, tails):
    packets[...] = jnp.zeros_like(packets)
    tails[...] = jnp.zeros_like(tails)
    holders = packets.shape[0] // BLOCKS
    for h in range(holders):
        seen[h] = 0
    head_size = queries.shape[-1]
    base = place[0] * child_count
    row = lax.broadcasted_iota(jnp.int32, (ROWS, head_size), 0)
    pick_row = lax.broadcasted_iota(jnp.int32, pick.shape, 0)
    pick_col = lax.broadcasted_iota(jnp.int32, pick.shape, 1) % (holders * MOST)
    chosen = jnp.zeros(pick.shape, jnp.bool_)
    for c in range(child_count):
        parent = child_parent[base + c]
        holder = lax.div(parent, parents)
        rank = seen[holder]
        seen[holder] = rank + 1
        slot = holder * MOST + rank
        fresh = new_kv[c : c + 1, :].astype(jnp.float32)
        length = parent_len[parent]
        high, low = lax.div(length, 32).astype(jnp.float32), lax.rem(length, 32).astype(jnp.float32)
        at = row - rank * EXTRA_ROWS
        tail = jnp.where(at == 0, fresh[:, :head_size], fresh[:, head_size:])
        tail = jnp.where(at < 2, tail, jnp.where(at == 2, high, low))
        tails[holder] = jnp.where((at >= 0) & (at < EXTRA_ROWS), tail, tails[holder])
        packets[holder * BLOCKS + rank] = queries[c]
        chosen = chosen | ((pick_row == c) & (pick_col == slot))
    pick[...] = jnp.where(chosen, 1.0, 0.0).astype(pick.dtype)
    for h in range(holders):
        packets[h * BLOCKS + MOST] = tails[h].astype(packets.dtype)


def ahead_kernel(
    parents, child_count, slots, place, child_parent_in, cache_hbm, near, plan,
    child_parent, hits, near_sem, parent_sem,
):
    get_near = pltpu.make_async_copy(cache_hbm.at[pl.ds(0, near.shape[0])], near, near_sem)
    get_parent = pltpu.make_async_copy(child_parent_in, child_parent, parent_sem)
    get_parent.start()
    get_near.start()
    for i in range(parents * GROUP):
        plan[i] = slots
    for p in range(parents):
        plan[COUNTS + p] = 0
    get_parent.wait()
    held = slots // MOST * parents
    count = jnp.int32(0)
    for r in range(slots // MOST):
        for c in range(child_count):
            parent = child_parent[r * child_count + c]
            hits[count] = parent + r * held
            count = count + (lax.div(parent, parents) == place[0]).astype(jnp.int32)

    def sort(i, carry):
        extra, last, rank = carry
        rep, local = lax.div(hits[i], held), lax.rem(hits[i], parents)
        rank = jnp.where(rep == last, rank + 1, 0)
        slot = rep * MOST + rank
        before = plan[COUNTS + local]
        plan[COUNTS + local] = before + 1
        fits = before < GROUP
        plan[jnp.where(fits, local * GROUP + before, EXTRAS + extra)] = jnp.where(fits, slot, slot * parents + local)
        return extra + jnp.where(fits, 0, 1), rep, rank

    start = (jnp.int32(0), jnp.int32(-1), jnp.int32(0))
    plan[EXTRA_COUNT] = lax.fori_loop(0, count, sort, start)[0]
    get_near.wait()


def unpack(packets, slot):
    holder, rank = lax.div(slot, MOST), lax.rem(slot, MOST)
    query = packets[holder * BLOCKS + rank].astype(jnp.float32)
    tail = packets[holder * BLOCKS + MOST].astype(jnp.float32)
    rows = [
        jnp.where(rank == 0, tail[i : i + 1], tail[i + EXTRA_ROWS : i + EXTRA_ROWS + 1]) for i in range(EXTRA_ROWS)
    ]
    return query, rows


def attend(packet_lists, keys, values, group):
    head_size = keys[0].shape[1]
    scale = head_size ** (-0.5) * LOG2_E

    def row_of(child, i):
        return jnp.broadcast_to(child[1][i], (group, head_size))

    wide = packet_lists
    query = [jnp.concatenate([w[0] for w in ws], axis=0) for ws in wide]
    scores = [
        lax.dot_general(q.astype(jnp.bfloat16), k, (((1,), (1,)), ((), ())), preferred_element_type=jnp.float32)
        for q, k in zip(query, keys)
    ]
    new_key = [jnp.concatenate([row_of(w, 0) for w in ws], axis=0) for ws in wide]
    new_score = [jnp.sum(q * k, axis=1, keepdims=True) for q, k in zip(query, new_key)]
    column = lax.broadcasted_iota(jnp.int32, (group, scores[0].shape[1]), 1).astype(jnp.float32)
    bias = [jnp.where(column < row_of(ws[0], 2)[:, :1] * 32.0 + row_of(ws[0], 3)[:, :1], 0.0, -jnp.inf) for ws in wide]
    scores = [s + jnp.concatenate([b] * len(ws), axis=0) for s, b, ws in zip(scores, bias, wide)]
    top = [jnp.maximum(jnp.max(s, axis=1, keepdims=True), x) for s, x in zip(scores, new_score)]
    weights = [jnp.exp2((s - t) * scale) for s, t in zip(scores, top)]
    summed = [
        jnp.dot(w.astype(jnp.bfloat16), v, preferred_element_type=jnp.float32) for w, v in zip(weights, values)
    ]
    new_weight = [jnp.exp2((x - t) * scale) for x, t in zip(new_score, top)]
    total = [jnp.sum(w, axis=1, keepdims=True) + x for w, x in zip(weights, new_weight)]
    new_value = [jnp.concatenate([row_of(w, 1) for w in ws], axis=0) for ws in wide]
    return [
        (s + x.astype(jnp.bfloat16).astype(jnp.float32) * v) / t
        for s, x, v, t in zip(summed, new_weight, new_value, total)
    ]


def attend_kernel(
    parents, plan_in, packets, near, cache_hbm, weight_hbm, out,
    plan, far, weight, heads, plan_sem, far_sem, weight_sems,
):
    slots = packets.shape[0] // BLOCKS * MOST
    group, head_size = packets.shape[1:]
    part = out.shape[1]
    parts = out.shape[0] // slots
    near_count = near.shape[0]
    get_far = pltpu.make_async_copy(cache_hbm.at[pl.ds(near_count, parents - near_count)], far, far_sem)
    bounds = [(cut * part, after * part) for cut, after in zip(CUTS, CUTS[1:])]
    get_weight = [
        pltpu.make_async_copy(
            weight_hbm.at[:, pl.ds(cut, after - cut)], weight.at[:, pl.ds(cut, after - cut)], weight_sems.at[i]
        )
        for i, (cut, after) in enumerate(bounds)
    ]
    get_plan = pltpu.make_async_copy(plan_in, plan, plan_sem)
    get_plan.start()
    get_far.start()
    for copy in get_weight:
        copy.start(priority=1)
    get_plan.wait()
    heads[...] = jnp.zeros_like(heads)

    def block(p):
        return (near, p) if p < near_count else (far, p - near_count)

    for some in STAGES:
        if some[-1] == parents - 1:
            get_far.wait()
        places = [[plan[p * GROUP + k] for k in range(GROUP)] for p in some]
        results = attend(
            [[unpack(packets, jnp.minimum(at, slots - 1)) for at in spots] for spots in places],
            [block(p)[0][block(p)[1], :, :head_size] for p in some],
            [block(p)[0][block(p)[1], :, head_size:] for p in some],
            group,
        )
        for spots, result in zip(places, results):
            for k, at in enumerate(spots):
                heads[pl.ds(pl.multiple_of(at * group, group), group), :] = result[k * group : (k + 1) * group]
    def one(keys, at):
        return attend([[unpack(packets, at)]], [keys[:, :head_size]], [keys[:, head_size:]], group)[0]

    def extra(i, carry):
        at, local = lax.div(plan[EXTRAS + i], parents), lax.rem(plan[EXTRAS + i], parents)
        rows = pl.ds(pl.multiple_of(at * group, group), group)

        @pl.when(local < near_count)
        def _():
            heads[rows, :] = one(near[jnp.minimum(local, near_count - 1)], at)

        @pl.when(local >= near_count)
        def _():
            heads[rows, :] = one(far[jnp.maximum(local - near_count, 0)], at)

        return carry

    lax.fori_loop(0, plan[EXTRA_COUNT], extra, 0)
    left = jnp.concatenate(
        [heads[pl.ds(i, slots, stride=group), :].astype(jnp.bfloat16) for i in range(group)], axis=1
    )
    for copy, (cut, after) in zip(get_weight, bounds):
        copy.wait()
        for low in range(cut, after, WIDE * part):
            sums = jnp.dot(left, weight[:, low : low + WIDE * part], preferred_element_type=jnp.float32).astype(out.dtype)
            for i in range(WIDE):
                first = (low // part + i) * slots
                out[first : first + slots, :] = sums[:, i * part : (i + 1) * part]


def shards(queries, new_kv, parent_cache, parent_len, child_parent, out_weight):
    reps = lax.axis_size("rep")
    tps = lax.axis_size("tp")
    parents, _, cache_len, width = parent_cache.shape
    child_count, group, head_size = queries.shape
    features = out_weight.shape[1]
    slots = reps * MOST
    place = lax.axis_index("rep").astype(jnp.int32).reshape(1)
    smem = pl.BlockSpec(memory_space=pltpu.SMEM)
    vmem = pl.BlockSpec(memory_space=pltpu.VMEM)
    anywhere = pl.BlockSpec(memory_space=pl.ANY)

    packets, pick = pl.pallas_call(
        functools.partial(pack_kernel, parents, child_count),
        out_shape=(
            jax.ShapeDtypeStruct((reps * BLOCKS, ROWS, head_size), jnp.bfloat16),
            jax.ShapeDtypeStruct((child_count, tps * slots), jnp.bfloat16),
        ),
        in_specs=[smem, smem, smem, vmem, vmem],
        out_specs=(vmem, vmem),
        scratch_shapes=[pltpu.SMEM((reps,), jnp.int32), pltpu.VMEM((reps, ROWS, head_size), jnp.float32)],
    )(place, child_parent, parent_len, queries, new_kv.reshape(child_count, width))
    packets = lax.all_to_all(packets, "rep", split_axis=0, concat_axis=0, tiled=True)

    caches = parent_cache.reshape(parents, cache_len, width)
    near, plan = pl.pallas_call(
        functools.partial(ahead_kernel, parents, child_count, slots),
        out_shape=(
            jax.ShapeDtypeStruct((NEAR, cache_len, width), caches.dtype),
            jax.ShapeDtypeStruct((PLAN,), jnp.int32),
        ),
        in_specs=[smem, anywhere, anywhere],
        out_specs=(vmem, smem),
        scratch_shapes=[
            pltpu.SMEM(child_parent.shape, jnp.int32),
            pltpu.SMEM((slots + 1,), jnp.int32),
            pltpu.SemaphoreType.DMA,
            pltpu.SemaphoreType.DMA,
        ],
        compiler_params=pltpu.CompilerParams(vmem_limit_bytes=50 * MIB),
        cost_estimate=pl.CostEstimate(flops=0, bytes_accessed=8 * MIB, transcendentals=0),
    )(place, child_parent, caches)

    partial = pl.pallas_call(
        functools.partial(attend_kernel, parents),
        out_shape=jax.ShapeDtypeStruct((tps * slots, features // tps), jnp.bfloat16),
        in_specs=[anywhere, vmem, vmem, anywhere, anywhere],
        out_specs=vmem,
        scratch_shapes=[
            pltpu.SMEM((PLAN,), jnp.int32),
            pltpu.VMEM((parents - NEAR, cache_len, width), jnp.bfloat16),
            pltpu.VMEM(out_weight.shape, jnp.bfloat16),
            pltpu.VMEM(((slots + 1) * group, head_size), jnp.float32),
            pltpu.SemaphoreType.DMA,
            pltpu.SemaphoreType.DMA,
            pltpu.SemaphoreType.DMA((len(CUTS) - 1,)),
        ],
        compiler_params=pltpu.CompilerParams(vmem_limit_bytes=50 * MIB),
    )(plan, packets, near, caches, out_weight)

    arrived = lax.all_to_all(partial, ("tp", "rep"), split_axis=0, concat_axis=0, tiled=True)
    return jnp.dot(pick, arrived, preferred_element_type=jnp.float32).astype(jnp.bfloat16)


def solution(mesh):
    placed = (
        P("rep", "tp", None),
        P("rep", "tp", None),
        P("rep", "tp", None, None),
        P(),
        P(),
        P("tp", None),
    )
    return jax.shard_map(
        shards, mesh=mesh, in_specs=placed, out_specs=P("rep", "tp"), check_vma=False
    )
```
